1024 devices in a mesh: node: 2 (over x_hi), shard: 64 (over z, x_lo), rep: 8 (over y, core).
Axes of the slice: x: 4 (x_hi: 2, x_lo: 2; x = x_hi * 2 + x_lo), y: 4, z: 32, core: 2. Of those that a mesh axis runs over, the one named last changes fastest.
Arguments:
- activations: bfloat16 [262144, 4096], P(('node', 'shard', 'rep')), may hold values from -24 to 24
- weight_codes: bfloat16 [4096, 512], P(('node', 'shard')), may hold values from -127 to 127
- block_scales: bfloat16 [4096, 4], P(('node', 'shard')), may hold values from 9.9658966e-05 to 0.00039863586
- cotangent: bfloat16 [262144, 512], P(('node', 'shard', 'rep')), may hold values from -6 to 6
Outputs:
- projected: bfloat16 [262144, 512], P(('node', 'shard', 'rep'))
- weight_grads: float32 [4096, 512], P(('node', 'shard'))
The draws below stay inside these ranges and needn't reach their ends.
All inputs are finite; a program needn't handle non-finite values.
Results may differ from the reference program's by a relative error of at most 0.015.
Values may be sent and summed in bfloat16 or wider, within the bound.
No kernel may reach another device: no remote copies, remote signals or barrier semaphores. Data moves between devices by JAX's collectives and lax.ppermute only.
A program may use at most 32 MiB of HBM per device.

```python
import math
import jax
import jax.numpy as jnp
from jax import lax

D_IN = 4096
KV_OUT = 512
BLOCK = 128
TOK_DEV = 256
TOKENS = 262144
N_NODE = 2
N_SHARD = 64
N_REP = 8


def draw_weight_codes(key, part):
    key = jax.random.fold_in(key, 7)
    whole = jax.random.randint(key, (D_IN, KV_OUT), -127, 128)
    return whole.astype(jnp.float32).astype(jnp.bfloat16)


def raised(values, rng, source, target, shards_of, factor):
    owner, partner = [(jnp.arange(values.shape[dim]) // (values.shape[dim] // shards_of)).reshape([-1 if axis == dim else 1 for axis in range(values.ndim)]) for dim in (source, target)]
    chosen = jax.random.permutation(rng, shards_of)[partner]
    strong = (owner == chosen) | (owner == (partner + shards_of // 2) % shards_of)
    return jnp.where(strong, factor * values, values)


def block_scale(own_key, shape, cuts, low, high):
    def one(position, parts):
        steps = jax.random.uniform(jax.random.fold_in(jax.random.fold_in(own_key, 6), position), (parts,), jnp.float32, low / len(cuts), high / len(cuts))
        return jnp.repeat(jnp.exp(steps), shape[position] // parts).reshape((-1,) + (1,) * (len(shape) - position - 1))

    level = one(*cuts[0])
    for cut in cuts[1:]:
        level = level * one(*cut)
    return level


def noise(rng, dims, scale, bound, cuts=(), dtype=jnp.bfloat16):
    result = scale * jax.random.normal(rng, dims, jnp.float32)
    if cuts:
        result = result * block_scale(rng, dims, cuts, -0.22, 0.18)
    return jnp.clip(result, -bound, bound).astype(dtype)


def bell_draw_with(key, extent, scale, most, shards, heavy, kind=jnp.bfloat16):
    array = scale * jax.random.normal(key, extent, jnp.float32)
    if shards:
        array = array * block_scale(key, extent, shards, -0.22, 0.18)
    return jnp.clip(raised(array, jax.random.fold_in(key, 3), *heavy), -most, most).astype(kind)


def setup_inputs(seed: int = 0) -> dict:
    streams_of = jax.random.split(jax.random.key(seed), 5)
    return {
        "activations": bell_draw_with(streams_of[0], (TOKENS, D_IN), 1.0, 24.0, ((0, 1024),), (0, 1, 1024, 6.0)),
        "weight_codes": draw_weight_codes(jax.random.fold_in(streams_of[4], 71), 0),
        "block_scales": jnp.clip(jnp.exp(math.log(0.00039863586) - 1.3862944 * jax.random.uniform(streams_of[2], (D_IN, KV_OUT // BLOCK), jnp.float32) ** block_scale(streams_of[2], (D_IN, KV_OUT // BLOCK), ((0, 128),), -0.2, 0.2)), 9.965896606445312e-05, 0.00039863586).astype(jnp.bfloat16),
        "cotangent": noise(streams_of[3], (TOKENS, KV_OUT), 1.0, 6.0, ((0, 1024),)),
    }


def dequantize(weight_codes, block_scales):
    widened = jnp.repeat(block_scales.astype(jnp.float32), BLOCK, axis=1)
    return (weight_codes.astype(jnp.float32) * widened).astype(jnp.bfloat16)


def reference(activations, weight_codes, block_scales, cotangent):
    weight = dequantize(weight_codes, block_scales)
    projected = jnp.dot(activations, weight, preferred_element_type=jnp.float32).astype(jnp.bfloat16)
    factor = float(TOKENS) ** -0.5
    grouped_in = activations.reshape(N_NODE, N_SHARD * N_REP, TOK_DEV, D_IN)
    grouped_out = cotangent.reshape(N_NODE, N_SHARD * N_REP, TOK_DEV, KV_OUT)
    grouped_in = jnp.transpose(grouped_in, (1, 0, 2, 3))
    grouped_out = jnp.transpose(grouped_out, (1, 0, 2, 3))

    def add_group(total, pieces):
        inputs_here, outputs_here = pieces
        paired = jnp.zeros((D_IN, KV_OUT), jnp.float32)
        for level in range(N_NODE):
            local = lax.dot_general(inputs_here[level], outputs_here[level], (((0,), (0,)), ((), ())), preferred_element_type=jnp.float32)
            partial_grad = (local * factor).astype(jnp.bfloat16)
            paired = paired + partial_grad.astype(jnp.float32)
        paired = paired.astype(jnp.bfloat16)
        return total + paired.astype(jnp.float32), None

    weight_grads, unused = lax.scan(add_group, jnp.zeros((D_IN, KV_OUT), jnp.float32), (grouped_in, grouped_out))
    return projected, weight_grads
```

```python
import jax
import jax.numpy as jnp
from jax import lax
from jax.sharding import Mesh, PartitionSpec as P

BLOCK = 128
ALL = ("xh", "z", "xl", "y", "c")
PLANE = ("xh", "xl", "y")
SWAP = [(0, 1), (1, 0)]


def body(activations, weight_codes, block_scales, cotangent):
    f32, bf16 = jnp.float32, jnp.bfloat16
    c = lax.axis_index("c")
    y = lax.axis_index("y")
    tok, d_in = activations.shape
    own, cols = weight_codes.shape
    half = cols // 2
    rows = own // 4
    n_z = lax.axis_size("z")
    tokens = tok * n_z * 32
    factor = float(tokens) ** (-0.5)

    other_act = lax.ppermute(activations, "c", SWAP)
    my_cot = lax.dynamic_slice(cotangent, (0, c * half), (tok, half))
    send_cot = lax.dynamic_slice(cotangent, (0, (1 - c) * half), (tok, half))
    other_cot = lax.ppermute(send_cot, "c", SWAP)

    dims = (((0,), (0,)), ((), ()))
    acts = jnp.concatenate([activations, other_act], axis=0)
    cots = jnp.concatenate([my_cot, other_cot], axis=0)
    grad = lax.dot_general(acts, cots, dims, preferred_element_type=f32)
    grad = (grad * factor).astype(bf16)
    grad = grad.reshape(2, n_z, 2, 4, rows, half)
    grad = grad.transpose(0, 2, 3, 1, 4, 5).reshape(16, n_z * rows, half)
    moved = lax.all_to_all(grad, PLANE, split_axis=0, concat_axis=0, tiled=True)
    plane = jnp.sum(moved.astype(f32), axis=0).astype(bf16)
    plane = plane.reshape(n_z, rows, half)
    moved_z = lax.all_to_all(plane, "z", split_axis=0, concat_axis=0, tiled=True)
    piece = jnp.sum(moved_z.astype(f32), axis=0)
    pieces = lax.all_gather(piece, ("y", "c"), axis=0, tiled=False)
    pieces = pieces.reshape(4, 2, rows, half)
    weight_grads = pieces.transpose(0, 2, 1, 3).reshape(own, cols)

    blocks = half // BLOCK
    codes = lax.dynamic_slice(weight_codes, (y * rows, c * half), (rows, half))
    scales = lax.dynamic_slice(block_scales, (y * rows, c * blocks), (rows, blocks))
    wide = jnp.repeat(scales.astype(f32), BLOCK, axis=1)
    mine = (codes.astype(f32) * wide).astype(bf16)
    spread = jnp.broadcast_to(mine[None], (n_z, rows, half))
    col = lax.all_to_all(spread, "z", split_axis=0, concat_axis=0, tiled=True)
    spread = jnp.broadcast_to(col.reshape(1, n_z * rows, half), (16, n_z * rows, half))
    whole = lax.all_to_all(spread, PLANE, split_axis=0, concat_axis=0, tiled=True)
    whole = whole.reshape(2, 2, 4, n_z, rows, half)
    weight = whole.transpose(0, 3, 1, 2, 4, 5).reshape(d_in, half)

    proj = jnp.dot(acts, weight, preferred_element_type=f32).astype(bf16)
    got = lax.ppermute(proj[tok:], "c", SWAP)
    kept = proj[:tok]
    left = jnp.where(c == 0, kept, got)
    right = jnp.where(c == 0, got, kept)
    projected = jnp.concatenate([left, right], axis=1)
    return (projected, weight_grads)


def solution(mesh):
    fine = Mesh(mesh.devices.reshape(2, 32, 2, 4, 2), ALL)
    placed = (
        P(ALL, None),
        P(("xh", "z", "xl"), None),
        P(("xh", "z", "xl"), None),
        P(ALL, None),
    )
    return jax.shard_map(
        body,
        mesh=fine,
        in_specs=placed,
        out_specs=(P(ALL, None), P(("xh", "z", "xl"), None)),
        check_vma=False,
    )
```

```python
import jax
import jax.numpy as jnp
from jax import lax
from jax.sharding import Mesh, PartitionSpec as P

BLOCK = 128
ALL = ("xh", "z", "xl", "y", "c")
X = ("xh", "xl")
SWAP = [(0, 1), (1, 0)]


def around(value, shift):
    return lax.ppermute(value, X, [(i, (i + shift) % 4) for i in range(4)])


def pick(stack, index):
    return lax.dynamic_index_in_dim(stack, index, 0, keepdims=False)


def body(activations, weight_codes, block_scales, cotangent):
    f32, bf16 = jnp.float32, jnp.bfloat16
    c = lax.axis_index("c")
    y = lax.axis_index("y")
    x = lax.axis_index(X)
    tok, d_in = activations.shape
    own, cols = weight_codes.shape
    half = cols // 2
    rows = own // 4
    n_z = lax.axis_size("z")
    column = n_z * rows
    factor = float(tok * n_z * 32) ** (-0.5)

    other_act = lax.ppermute(activations, "c", SWAP)
    my_cot = lax.dynamic_slice(cotangent, (0, c * half), (tok, half))
    send_cot = lax.dynamic_slice(cotangent, (0, (1 - c) * half), (tok, half))
    other_cot = lax.ppermute(send_cot, "c", SWAP)

    blocks = half // BLOCK
    codes = lax.dynamic_slice(weight_codes, (y * rows, c * half), (rows, half))
    scales = lax.dynamic_slice(block_scales, (y * rows, c * blocks), (rows, blocks))
    wide = jnp.repeat(scales.astype(f32), BLOCK, axis=1)
    mine = (codes.astype(f32) * wide).astype(bf16)
    spread = jnp.broadcast_to(mine[None], (n_z, rows, half))
    col = lax.all_to_all(spread, "z", split_axis=0, concat_axis=0, tiled=True)

    dims = (((0,), (0,)), ((), ()))
    acts = jnp.concatenate([activations, other_act], axis=0)
    cots = jnp.concatenate([my_cot, other_cot], axis=0)
    grad = lax.dot_general(acts, cots, dims, preferred_element_type=f32)
    grad = (grad * factor).astype(bf16)
    grad = grad.reshape(2, n_z, 2, 4, rows, half)
    grad = grad.transpose(0, 2, 3, 1, 4, 5).reshape(4, 4, column, half)
    total = pick(grad, x).astype(f32)
    for shift in (1, 3, 2):
        total += around(pick(grad, (x + shift) % 4), shift).astype(f32)
    line = total.astype(bf16)

    both = jnp.concatenate(
        [line, jnp.broadcast_to(col.reshape(1, column, half), (4, column, half))], axis=1
    )
    both = lax.all_to_all(both, "y", split_axis=0, concat_axis=0, tiled=True)
    plane = jnp.sum(both[:, :column].astype(f32), axis=0).astype(bf16)
    moved = lax.all_to_all(
        plane.reshape(n_z, rows, half), "z", split_axis=0, concat_axis=0, tiled=True
    )
    piece = jnp.sum(moved.astype(f32), axis=0)
    pieces = jnp.broadcast_to(piece[None], (8, rows, half))
    pieces = lax.all_to_all(pieces, ("y", "c"), split_axis=0, concat_axis=0, tiled=True)
    pieces = pieces.reshape(4, 2, rows, half)
    weight_grads = pieces.transpose(0, 2, 1, 3).reshape(own, cols)

    slab = both[:, column:]
    held = {shift: around(slab, shift) for shift in (1, 3, 2)}
    stack = jnp.stack([slab, held[1], held[2], held[3]])
    whole = jnp.stack([pick(stack, (x - k) % 4) for k in range(4)])
    whole = whole.reshape(2, 2, 4, n_z, rows, half)
    weight = whole.transpose(0, 3, 1, 2, 4, 5).reshape(d_in, half)

    proj = jnp.dot(acts, weight, preferred_element_type=f32).astype(bf16)
    got = lax.ppermute(proj[tok:], "c", SWAP)
    kept = proj[:tok]
    left = jnp.where(c == 0, kept, got)
    right = jnp.where(c == 0, got, kept)
    projected = jnp.concatenate([left, right], axis=1)
    return (projected, weight_grads)


def solution(mesh):
    fine = Mesh(mesh.devices.reshape(2, 32, 2, 4, 2), ALL)
    placed = (
        P(ALL, None),
        P(("xh", "z", "xl"), None),
        P(("xh", "z", "xl"), None),
        P(ALL, None),
    )
    return jax.shard_map(
        body,
        mesh=fine,
        in_specs=placed,
        out_specs=(P(ALL, None), P(("xh", "z", "xl"), None)),
        check_vma=False,
    )
```

```python
import jax
import jax.numpy as jnp
from jax import lax
from jax.sharding import Mesh, PartitionSpec as P

BLOCK = 128
ALL = ("xh", "z", "xl", "y", "c")
X = ("xh", "xl")
SWAP = [(0, 1), (1, 0)]


def around(value, shift):
    return lax.ppermute(value, X, [(i, (i + shift) % 4) for i in range(4)])


def over_z(value, steps):
    def step(held):
        return lax.all_to_all(held, "z", split_axis=0, concat_axis=0, tiled=True)

    return lax.cond(steps > 0, step, lambda held: held, value)


def pick(stack, index):
    return lax.dynamic_index_in_dim(stack, index, 0, keepdims=False)


def body(activations, weight_codes, block_scales, cotangent):
    f32, bf16 = jnp.float32, jnp.bfloat16
    c = lax.axis_index("c")
    y = lax.axis_index("y")
    x = lax.axis_index(X)
    once = 1 + jnp.minimum(x, 0)
    tok, d_in = activations.shape
    own, cols = weight_codes.shape
    half = cols // 2
    rows = own // 4
    n_z = lax.axis_size("z")
    column = n_z * rows
    factor = float(tok * n_z * 32) ** (-0.5)

    other_act = lax.ppermute(activations, "c", SWAP)
    my_cot = lax.dynamic_slice(cotangent, (0, c * half), (tok, half))
    send_cot = lax.dynamic_slice(cotangent, (0, (1 - c) * half), (tok, half))
    other_cot = lax.ppermute(send_cot, "c", SWAP)

    blocks = half // BLOCK
    codes = lax.dynamic_slice(weight_codes, (y * rows, c * half), (rows, half))
    scales = lax.dynamic_slice(block_scales, (y * rows, c * blocks), (rows, blocks))
    wide = jnp.repeat(scales.astype(f32), BLOCK, axis=1)
    mine = (codes.astype(f32) * wide).astype(bf16)
    spread = jnp.broadcast_to(mine[None], (n_z, rows, half))

    dims = (((0,), (0,)), ((), ()))
    acts = jnp.concatenate([activations, other_act], axis=0)
    cots = jnp.concatenate([my_cot, other_cot], axis=0)
    grad = lax.dot_general(acts, cots, dims, preferred_element_type=f32)
    grad = (grad * factor).astype(bf16)
    grad = grad.reshape(2, n_z, 2, 4, rows, half)
    grad = grad.transpose(0, 2, 3, 1, 4, 5).reshape(4, 4, column, half)
    sends = [pick(grad, (x + shift) % 4) for shift in (2, 1, 3)]
    *sends, spread = lax.optimization_barrier((*sends, spread))
    parts = [around(send, shift) for send, shift in zip(sends, (2, 1, 3))]
    col = over_z(spread, once)
    *parts, col = lax.optimization_barrier((*parts, col))
    total = pick(grad, x).astype(f32)
    for part in parts:
        total += part.astype(f32)
    line = total.astype(bf16)

    both = jnp.concatenate(
        [line, jnp.broadcast_to(col.reshape(1, column, half), (4, column, half))], axis=1
    )
    both = lax.all_to_all(both, "y", split_axis=0, concat_axis=0, tiled=True)
    plane = jnp.sum(both[:, :column].astype(f32), axis=0).astype(bf16)
    slab = both[:, column:]
    slab, plane = lax.optimization_barrier((slab, plane))
    held = [around(slab, shift) for shift in (2, 1, 3)]
    moved = over_z(plane.reshape(n_z, rows, half), once)
    *held, moved = lax.optimization_barrier((*held, moved))
    piece = jnp.sum(moved.astype(f32), axis=0)
    pieces = jnp.broadcast_to(piece[None], (8, rows, half))
    pieces = lax.all_to_all(pieces, ("y", "c"), split_axis=0, concat_axis=0, tiled=True)
    pieces = pieces.reshape(4, 2, rows, half)
    weight_grads = pieces.transpose(0, 2, 1, 3).reshape(own, cols)

    two, one, three = held
    stack = jnp.stack([slab, one, two, three])
    whole = jnp.stack([pick(stack, (x - k) % 4) for k in range(4)])
    whole = whole.reshape(2, 2, 4, n_z, rows, half)
    weight = whole.transpose(0, 3, 1, 2, 4, 5).reshape(d_in, half)

    proj = jnp.dot(acts, weight, preferred_element_type=f32).astype(bf16)
    got = lax.ppermute(proj[tok:], "c", SWAP)
    kept = proj[:tok]
    left = jnp.where(c == 0, kept, got)
    right = jnp.where(c == 0, got, kept)
    projected = jnp.concatenate([left, right], axis=1)
    return (projected, weight_grads)


def solution(mesh):
    fine = Mesh(mesh.devices.reshape(2, 32, 2, 4, 2), ALL)
    placed = (
        P(ALL, None),
        P(("xh", "z", "xl"), None),
        P(("xh", "z", "xl"), None),
        P(ALL, None),
    )
    return jax.shard_map(
        body,
        mesh=fine,
        in_specs=placed,
        out_specs=(P(ALL, None), P(("xh", "z", "xl"), None)),
        check_vma=False,
    )
```

```python
import jax
import jax.numpy as jnp
from jax import lax
from jax.sharding import Mesh, PartitionSpec as P

BLOCK = 128
ALL = ("xh", "z", "xl", "y", "c")
X = ("xh", "xl")
SWAP = [(0, 1), (1, 0)]


def around(value, shift):
    return lax.ppermute(value, X, [(i, (i + shift) % 4) for i in range(4)])


def pick(stack, index):
    return lax.dynamic_index_in_dim(stack, index, 0, keepdims=False)


def body(activations, weight_codes, block_scales, cotangent):
    f32, bf16 = jnp.float32, jnp.bfloat16
    c = lax.axis_index("c")
    y = lax.axis_index("y")
    x = lax.axis_index(X)
    tok, d_in = activations.shape
    own, cols = weight_codes.shape
    half = cols // 2
    rows = own // 4
    n_z = lax.axis_size("z")
    column = n_z * rows
    factor = float(tok * n_z * 32) ** (-0.5)

    other_act = lax.ppermute(activations, "c", SWAP)
    my_cot = lax.dynamic_slice(cotangent, (0, c * half), (tok, half))
    send_cot = lax.dynamic_slice(cotangent, (0, (1 - c) * half), (tok, half))
    other_cot = lax.ppermute(send_cot, "c", SWAP)

    blocks = half // BLOCK
    codes = lax.dynamic_slice(weight_codes, (y * rows, c * half), (rows, half))
    scales = lax.dynamic_slice(block_scales, (y * rows, c * blocks), (rows, blocks))
    wide = jnp.repeat(scales.astype(f32), BLOCK, axis=1)
    mine = (codes.astype(f32) * wide).astype(bf16)
    spread = jnp.broadcast_to(mine[None], (n_z, rows, half))

    dims = (((0,), (0,)), ((), ()))
    acts = jnp.concatenate([activations, other_act], axis=0)
    cots = jnp.concatenate([my_cot, other_cot], axis=0)
    grad = lax.dot_general(acts, cots, dims, preferred_element_type=f32)
    grad = (grad * factor).astype(bf16)
    grad = grad.reshape(2, n_z, 2, 4, rows, half)
    grad = grad.transpose(0, 2, 3, 1, 4, 5).reshape(4, 4, column, half)
    sends = [pick(grad, (x + shift) % 4) for shift in (2, 1, 3)]
    parts = [around(send, shift) for send, shift in zip(sends, (2, 1, 3))]
    turned = [[(k + n_z // 2) % n_z for k in range(n_z)]]
    col = lax.all_to_all(
        spread, "z", split_axis=0, concat_axis=0, axis_index_groups=turned, tiled=True
    )
    col = jnp.roll(col, n_z // 2, axis=0)
    total = pick(grad, x).astype(f32)
    for part in parts:
        total += part.astype(f32)
    line = total.astype(bf16)

    both = jnp.concatenate(
        [line, jnp.broadcast_to(col.reshape(1, column, half), (4, column, half))], axis=1
    )
    both = lax.all_to_all(both, "y", split_axis=0, concat_axis=0, tiled=True)
    plane = jnp.sum(both[:, :column].astype(f32), axis=0).astype(bf16)
    slab = both[:, column:]
    held = [around(slab, shift) for shift in (2, 1, 3)]
    moved = lax.all_to_all(
        plane.reshape(n_z, rows, half), "z", split_axis=0, concat_axis=0, tiled=True
    )
    *held, moved = lax.optimization_barrier((*held, moved))
    piece = jnp.sum(moved.astype(f32), axis=0)
    pieces = jnp.broadcast_to(piece[None], (8, rows, half))
    pieces = lax.all_to_all(pieces, ("y", "c"), split_axis=0, concat_axis=0, tiled=True)
    pieces = pieces.reshape(4, 2, rows, half)
    weight_grads = pieces.transpose(0, 2, 1, 3).reshape(own, cols)

    two, one, three = held
    stack = jnp.stack([slab, one, two, three])
    whole = jnp.stack([pick(stack, (x - k) % 4) for k in range(4)])
    whole = whole.reshape(2, 2, 4, n_z, rows, half)
    weight = whole.transpose(0, 3, 1, 2, 4, 5).reshape(d_in, half)

    proj = jnp.dot(acts, weight, preferred_element_type=f32).astype(bf16)
    got = lax.ppermute(proj[tok:], "c", SWAP)
    kept = proj[:tok]
    left = jnp.where(c == 0, kept, got)
    right = jnp.where(c == 0, got, kept)
    projected = jnp.concatenate([left, right], axis=1)
    return (projected, weight_grads)


def solution(mesh):
    fine = Mesh(mesh.devices.reshape(2, 32, 2, 4, 2), ALL)
    placed = (
        P(ALL, None),
        P(("xh", "z", "xl"), None),
        P(("xh", "z", "xl"), None),
        P(ALL, None),
    )
    return jax.shard_map(
        body,
        mesh=fine,
        in_specs=placed,
        out_specs=(P(ALL, None), P(("xh", "z", "xl"), None)),
        check_vma=False,
    )
```

```python
import jax
import jax.numpy as jnp
from jax import lax
from jax.sharding import Mesh, PartitionSpec as P

BLOCK = 128
ALL = ("xh", "z", "xl", "y", "c")
X = ("xh", "xl")
SWAP = [(0, 1), (1, 0)]


def around(value, shift):
    return lax.ppermute(value, X, [(i, (i + shift) % 4) for i in range(4)])


def over_z(value):
    n = value.shape[0]
    turned = [[(k + n // 2) % n for k in range(n)]]
    return lax.all_to_all(
        value, "z", split_axis=0, concat_axis=0, axis_index_groups=turned, tiled=True
    )


def pick(stack, index):
    return lax.dynamic_index_in_dim(stack, index, 0, keepdims=False)


def body(activations, weight_codes, block_scales, cotangent):
    f32, bf16 = jnp.float32, jnp.bfloat16
    c = lax.axis_index("c")
    y = lax.axis_index("y")
    x = lax.axis_index(X)
    tok, d_in = activations.shape
    own, cols = weight_codes.shape
    half = cols // 2
    rows = own // 4
    n_z = lax.axis_size("z")
    column = n_z * rows
    factor = float(tok * n_z * 32) ** (-0.5)

    other_act = lax.ppermute(activations, "c", SWAP)
    my_cot = lax.dynamic_slice(cotangent, (0, c * half), (tok, half))
    send_cot = lax.dynamic_slice(cotangent, (0, (1 - c) * half), (tok, half))
    other_cot = lax.ppermute(send_cot, "c", SWAP)

    blocks = half // BLOCK
    codes = lax.dynamic_slice(weight_codes, (y * rows, c * half), (rows, half))
    scales = lax.dynamic_slice(block_scales, (y * rows, c * blocks), (rows, blocks))
    wide = jnp.repeat(scales.astype(f32), BLOCK, axis=1)
    mine = (codes.astype(f32) * wide).astype(bf16)
    spread = jnp.broadcast_to(mine[None], (n_z, rows, half))

    dims = (((0,), (0,)), ((), ()))
    acts = jnp.concatenate([activations, other_act], axis=0)
    cots = jnp.concatenate([my_cot, other_cot], axis=0)
    grad = lax.dot_general(acts, cots, dims, preferred_element_type=f32)
    grad = (grad * factor).astype(bf16)
    grad = grad.reshape(2, n_z, 2, 4, rows, half)
    grad = grad.transpose(0, 2, 3, 1, 4, 5).reshape(4, 4, column, half)
    sends = [pick(grad, (x + shift) % 4) for shift in (2, 1, 3)]
    *sends, spread = lax.optimization_barrier((*sends, spread))
    parts = [around(send, shift) for send, shift in zip(sends, (2, 1, 3))]
    col = lax.cond(x >= 0, over_z, lambda held: held, spread)
    *parts, col = lax.optimization_barrier((*parts, col))
    col = jnp.roll(col, n_z // 2, axis=0)
    total = pick(grad, x).astype(f32)
    for part in parts:
        total += part.astype(f32)
    line = total.astype(bf16)

    both = jnp.concatenate(
        [line, jnp.broadcast_to(col.reshape(1, column, half), (4, column, half))], axis=1
    )
    both = lax.all_to_all(both, "y", split_axis=0, concat_axis=0, tiled=True)
    plane = jnp.sum(both[:, :column].astype(f32), axis=0).astype(bf16)
    slab = both[:, column:]
    held = [around(slab, shift) for shift in (2, 1, 3)]
    moved = over_z(jnp.roll(plane.reshape(n_z, rows, half), n_z // 2, axis=0))

    two, one, three = held
    stack = jnp.stack([slab, one, two, three])
    whole = jnp.stack([pick(stack, (x - k) % 4) for k in range(4)])
    whole = whole.reshape(2, 2, 4, n_z, rows, half)
    weight = whole.transpose(0, 3, 1, 2, 4, 5).reshape(d_in, half)

    proj = jnp.dot(acts, weight, preferred_element_type=f32).astype(bf16)
    proj, moved = lax.optimization_barrier((proj, moved))
    piece = jnp.sum(moved.astype(f32), axis=0)
    pieces = jnp.broadcast_to(piece[None], (8, rows, half))
    pieces = lax.all_to_all(pieces, ("y", "c"), split_axis=0, concat_axis=0, tiled=True)
    pieces = pieces.reshape(4, 2, rows, half)
    weight_grads = pieces.transpose(0, 2, 1, 3).reshape(own, cols)

    got = lax.ppermute(proj[tok:], "c", SWAP)
    kept = proj[:tok]
    left = jnp.where(c == 0, kept, got)
    right = jnp.where(c == 0, got, kept)
    projected = jnp.concatenate([left, right], axis=1)
    return (projected, weight_grads)


def solution(mesh):
    fine = Mesh(mesh.devices.reshape(2, 32, 2, 4, 2), ALL)
    placed = (
        P(ALL, None),
        P(("xh", "z", "xl"), None),
        P(("xh", "z", "xl"), None),
        P(ALL, None),
    )
    return jax.shard_map(
        body,
        mesh=fine,
        in_specs=placed,
        out_specs=(P(ALL, None), P(("xh", "z", "xl"), None)),
        check_vma=False,
    )
```

```python
import jax
import jax.numpy as jnp
from jax import lax
from jax.sharding import Mesh, PartitionSpec as P

BLOCK = 128
ALL = ("xh", "z", "xl", "y", "c")
X = ("xh", "xl")
SWAP = [(0, 1), (1, 0)]


def around(value, axes, shift):
    return lax.ppermute(value, axes, [(i, (i + shift) % 4) for i in range(4)])


def spread_sum(stack, axes):
    me = lax.axis_index(axes)
    parts = [around(pick(stack, (me + shift) % 4), axes, shift) for shift in (2, 1, 3)]
    total = pick(stack, me).astype(jnp.float32)
    for part in parts:
        total += part.astype(jnp.float32)
    return total.astype(stack.dtype)


def over_z(value):
    n = value.shape[0]
    turned = [[(k + n // 2) % n for k in range(n)]]
    return lax.all_to_all(
        value, "z", split_axis=0, concat_axis=0, axis_index_groups=turned, tiled=True
    )


def pick(stack, index):
    return lax.dynamic_index_in_dim(stack, index, 0, keepdims=False)


def body(activations, weight_codes, block_scales, cotangent):
    f32, bf16 = jnp.float32, jnp.bfloat16
    c = lax.axis_index("c")
    y = lax.axis_index("y")
    x = lax.axis_index(X)
    tok, d_in = activations.shape
    own, cols = weight_codes.shape
    half = cols // 2
    rows = own // 4
    n_z = lax.axis_size("z")
    column = n_z * rows
    factor = float(tok * n_z * 32) ** (-0.5)

    other_act = lax.ppermute(activations, "c", SWAP)
    my_cot = lax.dynamic_slice(cotangent, (0, c * half), (tok, half))
    send_cot = lax.dynamic_slice(cotangent, (0, (1 - c) * half), (tok, half))
    other_cot = lax.ppermute(send_cot, "c", SWAP)

    blocks = half // BLOCK
    codes = lax.dynamic_slice(weight_codes, (y * rows, c * half), (rows, half))
    scales = lax.dynamic_slice(block_scales, (y * rows, c * blocks), (rows, blocks))
    wide = jnp.repeat(scales.astype(f32), BLOCK, axis=1)
    mine = (codes.astype(f32) * wide).astype(bf16)
    spread = jnp.broadcast_to(mine[None], (n_z, rows, half))

    dims = (((0,), (0,)), ((), ()))
    acts = jnp.concatenate([activations, other_act], axis=0)
    cots = jnp.concatenate([my_cot, other_cot], axis=0)
    grad = lax.dot_general(acts, cots, dims, preferred_element_type=f32)
    grad = (grad * factor).astype(bf16)
    grad = grad.reshape(2, n_z, 2, 4, rows, half)
    grad = grad.transpose(0, 2, 3, 1, 4, 5).reshape(4, 4, column, half)
    grad, spread = lax.optimization_barrier((grad, spread))
    col = over_z(spread)
    plane = spread_sum(spread_sum(grad, X), "y")
    col, plane = lax.optimization_barrier((col, plane))
    col = jnp.roll(col, n_z // 2, axis=0)

    slab = jnp.broadcast_to(col.reshape(1, column, half), (4, column, half))
    slab = lax.all_to_all(slab, "y", split_axis=0, concat_axis=0, tiled=True)
    slab, plane = lax.optimization_barrier((slab, plane))
    held = [around(slab, X, shift) for shift in (2, 1, 3)]
    moved = over_z(jnp.roll(plane.reshape(n_z, rows, half), n_z // 2, axis=0))

    two, one, three = held
    stack = jnp.stack([slab, one, two, three])
    whole = jnp.stack([pick(stack, (x - k) % 4) for k in range(4)])
    whole = whole.reshape(2, 2, 4, n_z, rows, half)
    weight = whole.transpose(0, 3, 1, 2, 4, 5).reshape(d_in, half)

    proj = jnp.dot(acts, weight, preferred_element_type=f32).astype(bf16)
    got = lax.ppermute(proj[tok:], "c", SWAP)
    kept = proj[:tok]
    got, kept, moved = lax.optimization_barrier((got, kept, moved))
    piece = jnp.sum(moved.astype(f32), axis=0)
    pieces = jnp.broadcast_to(piece[None], (8, rows, half))
    pieces = lax.all_to_all(pieces, ("y", "c"), split_axis=0, concat_axis=0, tiled=True)
    pieces = pieces.reshape(4, 2, rows, half)
    weight_grads = pieces.transpose(0, 2, 1, 3).reshape(own, cols)

    left = jnp.where(c == 0, kept, got)
    right = jnp.where(c == 0, got, kept)
    projected = jnp.concatenate([left, right], axis=1)
    return (projected, weight_grads)


def solution(mesh):
    fine = Mesh(mesh.devices.reshape(2, 32, 2, 4, 2), ALL)
    placed = (
        P(ALL, None),
        P(("xh", "z", "xl"), None),
        P(("xh", "z", "xl"), None),
        P(ALL, None),
    )
    return jax.shard_map(
        body,
        mesh=fine,
        in_specs=placed,
        out_specs=(P(ALL, None), P(("xh", "z", "xl"), None)),
        check_vma=False,
    )
```

```python
import jax
import jax.numpy as jnp
from jax import lax
from jax.sharding import Mesh, PartitionSpec as P

BLOCK = 128
ALL = ("xh", "z", "xl", "y", "c")
X = ("xh", "xl")
SWAP = [(0, 1), (1, 0)]


def around(value, axes, shift):
    return lax.ppermute(value, axes, [(i, (i + shift) % 4) for i in range(4)])


def spread_sum(piece, axes):
    me = lax.axis_index(axes)
    parts = [around(piece((me + shift) % 4), axes, shift) for shift in (2, 1, 3)]
    mine = piece(me)
    total = mine.astype(jnp.float32)
    for part in parts:
        total += part.astype(jnp.float32)
    return total.astype(mine.dtype)


def over_z(value, first):
    n = value.shape[0]
    turned = [[(k + first) % n for k in range(n)]]
    return lax.all_to_all(
        value, "z", split_axis=0, concat_axis=0, axis_index_groups=turned, tiled=True
    )


def pick(stack, index):
    return lax.dynamic_index_in_dim(stack, index, 0, keepdims=False)


def body(activations, weight_codes, block_scales, cotangent):
    f32, bf16 = jnp.float32, jnp.bfloat16
    c = lax.axis_index("c")
    y = lax.axis_index("y")
    x = lax.axis_index(X)
    tok, d_in = activations.shape
    own, cols = weight_codes.shape
    half = cols // 2
    rows = own // 4
    n_z = lax.axis_size("z")
    column = n_z * rows
    factor = float(tok * n_z * 32) ** (-0.5)

    other_act = lax.ppermute(activations, "c", SWAP)
    my_cot = lax.dynamic_slice(cotangent, (0, c * half), (tok, half))
    send_cot = lax.dynamic_slice(cotangent, (0, (1 - c) * half), (tok, half))
    other_cot = lax.ppermute(send_cot, "c", SWAP)

    blocks = half // BLOCK
    codes = lax.dynamic_slice(weight_codes, (y * rows, c * half), (rows, half))
    scales = lax.dynamic_slice(block_scales, (y * rows, c * blocks), (rows, blocks))
    wide = jnp.repeat(scales.astype(f32), BLOCK, axis=1)
    mine = (codes.astype(f32) * wide).astype(bf16)
    spread = jnp.broadcast_to(mine[None], (n_z, rows, half))

    dims = (((0,), (0,)), ((), ()))
    acts = jnp.concatenate([activations, other_act], axis=0)
    cots = jnp.concatenate([my_cot, other_cot], axis=0)
    grad = lax.dot_general(acts, cots, dims, preferred_element_type=f32)
    grad = (grad * factor).astype(bf16)
    grad = grad.reshape(2, n_z, 2, 4, rows, half)
    grad, spread = lax.optimization_barrier((grad, spread))
    first = 3 * n_z // 4
    col = over_z(spread, first)

    def to_x(k):
        start = (k // 2, 0, k % 2, 0, 0, 0)
        return lax.dynamic_slice(grad, start, (1, n_z, 1, 4, rows, half)).reshape(n_z, 4, rows, half)

    line = spread_sum(to_x, X)
    plane = spread_sum(lambda k: lax.dynamic_index_in_dim(line, k, 1, keepdims=False), "y")
    col, plane = lax.optimization_barrier((col, plane))
    col = jnp.roll(col, first, axis=0)

    slab = jnp.broadcast_to(col.reshape(1, column, half), (4, column, half))
    slab = lax.all_to_all(slab, "y", split_axis=0, concat_axis=0, tiled=True)
    slab, plane = lax.optimization_barrier((slab, plane))
    held = [around(slab, X, shift) for shift in (2, 1, 3)]
    moved = over_z(jnp.roll(plane, n_z // 2, axis=0), n_z // 2)

    two, one, three = held
    stack = jnp.stack([slab, one, two, three])
    whole = jnp.stack([pick(stack, (x - k) % 4) for k in range(4)])
    whole = whole.reshape(2, 2, 4, n_z, rows, half)
    weight = whole.transpose(0, 3, 1, 2, 4, 5).reshape(d_in, half)

    proj = jnp.dot(acts, weight, preferred_element_type=f32).astype(bf16)
    got = lax.ppermute(proj[tok:], "c", SWAP)
    kept = proj[:tok]
    got, kept, moved = lax.optimization_barrier((got, kept, moved))
    piece = jnp.sum(moved.astype(f32), axis=0)
    pieces = jnp.broadcast_to(piece[None], (8, rows, half))
    pieces = lax.all_to_all(pieces, ("y", "c"), split_axis=0, concat_axis=0, tiled=True)
    pieces = pieces.reshape(4, 2, rows, half)
    weight_grads = pieces.transpose(0, 2, 1, 3).reshape(own, cols)

    left = jnp.where(c == 0, kept, got)
    right = jnp.where(c == 0, got, kept)
    projected = jnp.concatenate([left, right], axis=1)
    return (projected, weight_grads)


def solution(mesh):
    fine = Mesh(mesh.devices.reshape(2, 32, 2, 4, 2), ALL)
    placed = (
        P(ALL, None),
        P(("xh", "z", "xl"), None),
        P(("xh", "z", "xl"), None),
        P(ALL, None),
    )
    return jax.shard_map(
        body,
        mesh=fine,
        in_specs=placed,
        out_specs=(P(ALL, None), P(("xh", "z", "xl"), None)),
        check_vma=False,
    )
```

```python
import jax
import jax.numpy as jnp
from jax import lax
from jax.sharding import Mesh, PartitionSpec as P

BLOCK = 128
ALL = ("xh", "z", "xl", "y", "c")
X = ("xh", "xl")
SWAP = [(0, 1), (1, 0)]


def around(value, axes, shift):
    return lax.ppermute(value, axes, [(i, (i + shift) % 4) for i in range(4)])


def spread_sum(piece, axes):
    me = lax.axis_index(axes)
    parts = [around(piece((me + shift) % 4), axes, shift) for shift in (2, 1, 3)]
    mine = piece(me)
    total = mine.astype(jnp.float32)
    for part in parts:
        total += part.astype(jnp.float32)
    return total.astype(mine.dtype)


def over_z(value, first):
    n = value.shape[0]
    turned = [[(k + first) % n for k in range(n)]]
    return lax.all_to_all(
        value, "z", split_axis=0, concat_axis=0, axis_index_groups=turned, tiled=True
    )


def pick(stack, index):
    return lax.dynamic_index_in_dim(stack, index, 0, keepdims=False)


def body(activations, weight_codes, block_scales, cotangent):
    f32, bf16 = jnp.float32, jnp.bfloat16
    c = lax.axis_index("c")
    y = lax.axis_index("y")
    x = lax.axis_index(X)
    tok, d_in = activations.shape
    own, cols = weight_codes.shape
    half = cols // 2
    rows = own // 4
    n_z = lax.axis_size("z")
    column = n_z * rows
    factor = float(tok * n_z * 32) ** (-0.5)

    other_act = lax.ppermute(activations, "c", SWAP)
    my_cot = lax.dynamic_slice(cotangent, (0, c * half), (tok, half))
    send_cot = lax.dynamic_slice(cotangent, (0, (1 - c) * half), (tok, half))
    other_cot = lax.ppermute(send_cot, "c", SWAP)

    blocks = half // BLOCK
    codes = lax.dynamic_slice(weight_codes, (y * rows, c * half), (rows, half))
    scales = lax.dynamic_slice(block_scales, (y * rows, c * blocks), (rows, blocks))
    wide = jnp.repeat(scales.astype(f32), BLOCK, axis=1)
    mine = (codes.astype(f32) * wide).astype(bf16)
    spread = jnp.broadcast_to(mine[None], (n_z, rows, half))

    dims = (((0,), (0,)), ((), ()))
    acts = jnp.concatenate([activations, other_act], axis=0)
    cots = jnp.concatenate([my_cot, other_cot], axis=0)
    grad = lax.dot_general(acts, cots, dims, preferred_element_type=f32)
    grad = (grad * factor).astype(bf16)
    grad = grad.reshape(2, n_z, 2, 4, rows, half)
    grad, spread = lax.optimization_barrier((grad, spread))
    first = 3 * n_z // 4
    col = over_z(spread, first)

    def to_x(k):
        start = (k // 2, 0, k % 2, 0, 0, 0)
        return lax.dynamic_slice(grad, start, (1, n_z, 1, 4, rows, half)).reshape(n_z, 4, rows, half)

    line = spread_sum(to_x, X)
    plane = spread_sum(lambda k: lax.dynamic_index_in_dim(line, k, 1, keepdims=False), "y")
    col, plane = lax.optimization_barrier((col, plane))
    col = jnp.roll(col, first, axis=0)

    slab = jnp.broadcast_to(col.reshape(1, column, half), (4, column, half))
    slab = lax.all_to_all(slab, "y", split_axis=0, concat_axis=0, tiled=True)
    slab, plane = lax.optimization_barrier((slab, plane))
    one, three = around(slab, X, 1), around(slab, X, 3)
    moved = over_z(jnp.roll(plane, n_z // 2, axis=0), n_z // 2)
    two = jnp.concatenate([around(one[:2], X, 1), around(three[2:], X, 3)])
    piece = jnp.sum(moved.astype(f32), axis=0)
    pieces = jnp.broadcast_to(piece[None], (8, rows, half))
    pieces = lax.all_to_all(pieces, ("y", "c"), split_axis=0, concat_axis=0, tiled=True)
    stack = jnp.stack([slab, one, two, three])
    whole = jnp.stack([pick(stack, (x - k) % 4) for k in range(4)])
    whole = whole.reshape(2, 2, 4, n_z, rows, half)
    weight = whole.transpose(0, 3, 1, 2, 4, 5).reshape(d_in, half)

    proj = jnp.dot(acts, weight, preferred_element_type=f32).astype(bf16)
    proj, pieces = lax.optimization_barrier((proj, pieces))
    pieces = pieces.reshape(4, 2, rows, half)
    weight_grads = pieces.transpose(0, 2, 1, 3).reshape(own, cols)

    got = lax.ppermute(proj[tok:], "c", SWAP)
    kept = proj[:tok]
    left = jnp.where(c == 0, kept, got)
    right = jnp.where(c == 0, got, kept)
    projected = jnp.concatenate([left, right], axis=1)
    return (projected, weight_grads)


def solution(mesh):
    fine = Mesh(mesh.devices.reshape(2, 32, 2, 4, 2), ALL)
    placed = (
        P(ALL, None),
        P(("xh", "z", "xl"), None),
        P(("xh", "z", "xl"), None),
        P(ALL, None),
    )
    return jax.shard_map(
        body,
        mesh=fine,
        in_specs=placed,
        out_specs=(P(ALL, None), P(("xh", "z", "xl"), None)),
        check_vma=False,
    )
```

```python
import jax
import jax.numpy as jnp
from jax import lax
from jax.sharding import Mesh, PartitionSpec as P

BLOCK = 128
ALL = ("xh", "z", "xl", "y", "c")
X = ("xh", "xl")
SWAP = [(0, 1), (1, 0)]


def around(value, axes, shift):
    return lax.ppermute(value, axes, [(i, (i + shift) % 4) for i in range(4)])


def spread_sum(piece, axes):
    me = lax.axis_index(axes)
    parts = [around(piece((me + shift) % 4), axes, shift) for shift in (2, 1, 3)]
    mine = piece(me)
    total = mine.astype(jnp.float32)
    for part in parts:
        total += part.astype(jnp.float32)
    return total.astype(mine.dtype)


def over_z(value, first):
    n = value.shape[0]
    turned = [[(k + first) % n for k in range(n)]]
    return lax.all_to_all(
        value, "z", split_axis=0, concat_axis=0, axis_index_groups=turned, tiled=True
    )


def pick(stack, index):
    return lax.dynamic_index_in_dim(stack, index, 0, keepdims=False)


def body(activations, weight_codes, block_scales, cotangent):
    f32, bf16 = jnp.float32, jnp.bfloat16
    c = lax.axis_index("c")
    y = lax.axis_index("y")
    x = lax.axis_index(X)
    tok, d_in = activations.shape
    own, cols = weight_codes.shape
    half = cols // 2
    rows = own // 4
    n_z = lax.axis_size("z")
    column = n_z * rows
    factor = float(tok * n_z * 32) ** (-0.5)

    other_act = lax.ppermute(activations, "c", SWAP)
    other_cot = lax.ppermute(cotangent, "c", SWAP)

    blocks = half // BLOCK
    codes = lax.dynamic_slice(weight_codes, (y * rows, c * half), (rows, half))
    scales = lax.dynamic_slice(block_scales, (y * rows, c * blocks), (rows, blocks))
    wide = jnp.repeat(scales.astype(f32), BLOCK, axis=1)
    mine = (codes.astype(f32) * wide).astype(bf16)
    spread = jnp.broadcast_to(mine[None], (n_z, rows, half))

    dims = (((0,), (0,)), ((), ()))
    acts = jnp.concatenate([activations, other_act], axis=0)
    cots = jnp.concatenate([cotangent, other_cot], axis=0)
    cots = lax.dynamic_slice(cots, (0, c * half), (2 * tok, half))
    grad = lax.dot_general(acts, cots, dims, preferred_element_type=f32)
    grad = (grad * factor).astype(bf16)
    grad = grad.reshape(2, n_z, 2, 4, rows, half)
    first = 3 * n_z // 4
    col = over_z(spread, first)

    def to_x(k):
        start = (k // 2, 0, k % 2, 0, 0, 0)
        return lax.dynamic_slice(grad, start, (1, n_z, 1, 4, rows, half)).reshape(n_z, 4, rows, half)

    line = spread_sum(to_x, X)
    plane = spread_sum(lambda k: lax.dynamic_index_in_dim(line, k, 1, keepdims=False), "y")
    col, plane = lax.optimization_barrier((col, plane))
    col = jnp.roll(col, first, axis=0)

    slab = jnp.broadcast_to(col.reshape(1, column, half), (4, column, half))
    slab = lax.all_to_all(slab, "y", split_axis=0, concat_axis=0, tiled=True)
    slab, plane = lax.optimization_barrier((slab, plane))
    held = [around(slab, X, shift) for shift in (2, 1, 3)]
    moved = over_z(jnp.roll(plane, n_z // 2, axis=0), n_z // 2)

    two, one, three = held
    stack = jnp.stack([slab, one, two, three])
    whole = jnp.stack([pick(stack, (x - k) % 4) for k in range(4)])
    whole = whole.reshape(2, 2, 4, n_z, rows, half)
    weight = whole.transpose(0, 3, 1, 2, 4, 5).reshape(d_in, half)

    proj = jnp.dot(acts, weight, preferred_element_type=f32).astype(bf16)
    got = lax.ppermute(proj[tok:], "c", SWAP)
    kept = proj[:tok]
    got, kept, moved = lax.optimization_barrier((got, kept, moved))
    piece = jnp.sum(moved.astype(f32), axis=0)
    pieces = jnp.broadcast_to(piece[None], (8, rows, half))
    pieces = lax.all_to_all(pieces, ("y", "c"), split_axis=0, concat_axis=0, tiled=True)
    pieces = pieces.reshape(4, 2, rows, half)
    weight_grads = pieces.transpose(0, 2, 1, 3).reshape(own, cols)

    left = jnp.where(c == 0, kept, got)
    right = jnp.where(c == 0, got, kept)
    projected = jnp.concatenate([left, right], axis=1)
    return (projected, weight_grads)


def solution(mesh):
    fine = Mesh(mesh.devices.reshape(2, 32, 2, 4, 2), ALL)
    placed = (
        P(ALL, None),
        P(("xh", "z", "xl"), None),
        P(("xh", "z", "xl"), None),
        P(ALL, None),
    )
    return jax.shard_map(
        body,
        mesh=fine,
        in_specs=placed,
        out_specs=(P(ALL, None), P(("xh", "z", "xl"), None)),
        check_vma=False,
    )
```

```python
import jax
import jax.numpy as jnp
from jax import lax
from jax.sharding import Mesh, PartitionSpec as P

BLOCK = 128
ALL = ("xh", "z", "xl", "y", "c")
X = ("xh", "xl")
SWAP = [(0, 1), (1, 0)]


def around(value, axes, shift):
    return lax.ppermute(value, axes, [(i, (i + shift) % 4) for i in range(4)])


def spread_sum(piece, axes):
    me = lax.axis_index(axes)
    parts = [around(piece((me + shift) % 4), axes, shift) for shift in (2, 1, 3)]
    mine = piece(me)
    total = mine.astype(jnp.float32)
    for part in parts:
        total += part.astype(jnp.float32)
    return total.astype(mine.dtype)


def over_z(value, first):
    n = value.shape[0]
    turned = [[(k + first) % n for k in range(n)]]
    return lax.all_to_all(
        value, "z", split_axis=0, concat_axis=0, axis_index_groups=turned, tiled=True
    )


def pick(stack, index):
    return lax.dynamic_index_in_dim(stack, index, 0, keepdims=False)


def body(activations, weight_codes, block_scales, cotangent):
    f32, bf16 = jnp.float32, jnp.bfloat16
    c = lax.axis_index("c")
    y = lax.axis_index("y")
    x = lax.axis_index(X)
    tok, d_in = activations.shape
    own, cols = weight_codes.shape
    half = cols // 2
    rows = own // 4
    n_z = lax.axis_size("z")
    column = n_z * rows
    factor = float(tok * n_z * 32) ** (-0.5)

    other_act = lax.ppermute(activations, "c", SWAP)
    other_cot = lax.ppermute(cotangent, "c", SWAP)

    blocks = half // BLOCK
    codes = lax.dynamic_slice(weight_codes, (y * rows, c * half), (rows, half))
    scales = lax.dynamic_slice(block_scales, (y * rows, c * blocks), (rows, blocks))
    wide = jnp.repeat(scales.astype(f32), BLOCK, axis=1)
    mine = (codes.astype(f32) * wide).astype(bf16)
    spread = jnp.broadcast_to(mine[None], (n_z, rows, half))

    dims = (((0,), (0,)), ((), ()))
    acts = jnp.concatenate([activations, other_act], axis=0)
    cots = jnp.concatenate([cotangent, other_cot], axis=0)
    cots = lax.dynamic_slice(cots, (0, c * half), (2 * tok, half))
    grad = lax.dot_general(acts, cots, dims, preferred_element_type=f32)
    grad = (grad * factor).astype(bf16)
    grad = grad.reshape(2, n_z, 2, 4, rows, half)
    first = 11 * n_z // 16
    col = over_z(spread, first)

    def to_x(k):
        start = (k // 2, 0, k % 2, 0, 0, 0)
        return lax.dynamic_slice(grad, start, (1, n_z, 1, 4, rows, half)).reshape(n_z, 4, rows, half)

    line = spread_sum(to_x, X)
    y_piece = lambda k: lax.dynamic_index_in_dim(line, k, 1, keepdims=False)
    parts = [around(y_piece((y + shift) % 4), "y", shift) for shift in (2, 1, 3)]
    col, parts[0], parts[1] = lax.optimization_barrier((col, parts[0], parts[1]))
    total = y_piece(y).astype(f32)
    for part in parts:
        total += part.astype(f32)
    plane = total.astype(bf16)
    col = jnp.roll(col, first, axis=0)

    slab = jnp.broadcast_to(col.reshape(1, column, half), (4, column, half))
    slab = lax.all_to_all(slab, "y", split_axis=0, concat_axis=0, tiled=True)
    slab, plane = lax.optimization_barrier((slab, plane))
    held = [around(slab, X, shift) for shift in (2, 1, 3)]
    moved = over_z(jnp.roll(plane, n_z // 2, axis=0), n_z // 2)

    two, one, three = held
    stack = jnp.stack([slab, one, two, three])
    whole = jnp.stack([pick(stack, (x - k) % 4) for k in range(4)])
    whole = whole.reshape(2, 2, 4, n_z, rows, half)
    weight = whole.transpose(0, 3, 1, 2, 4, 5).reshape(d_in, half)

    proj = jnp.dot(acts, weight, preferred_element_type=f32).astype(bf16)
    got = lax.ppermute(proj[tok:], "c", SWAP)
    kept = proj[:tok]
    got, kept, moved = lax.optimization_barrier((got, kept, moved))
    piece = jnp.sum(moved.astype(f32), axis=0)
    pieces = jnp.broadcast_to(piece[None], (8, rows, half))
    pieces = lax.all_to_all(pieces, ("y", "c"), split_axis=0, concat_axis=0, tiled=True)
    pieces = pieces.reshape(4, 2, rows, half)
    weight_grads = pieces.transpose(0, 2, 1, 3).reshape(own, cols)

    left = jnp.where(c == 0, kept, got)
    right = jnp.where(c == 0, got, kept)
    projected = jnp.concatenate([left, right], axis=1)
    return (projected, weight_grads)


def solution(mesh):
    fine = Mesh(mesh.devices.reshape(2, 32, 2, 4, 2), ALL)
    placed = (
        P(ALL, None),
        P(("xh", "z", "xl"), None),
        P(("xh", "z", "xl"), None),
        P(ALL, None),
    )
    return jax.shard_map(
        body,
        mesh=fine,
        in_specs=placed,
        out_specs=(P(ALL, None), P(("xh", "z", "xl"), None)),
        check_vma=False,
    )
```

```python
import jax
import jax.numpy as jnp
from jax import lax
from jax.sharding import Mesh, PartitionSpec as P

BLOCK = 128
ALL = ("xh", "z", "xl", "y", "c")
X = ("xh", "xl")
SWAP = [(0, 1), (1, 0)]


def around(value, axes, shift):
    return lax.ppermute(value, axes, [(i, (i + shift) % 4) for i in range(4)])


def spread_sum(piece, axes):
    me = lax.axis_index(axes)
    parts = [around(piece((me + shift) % 4), axes, shift) for shift in (2, 1, 3)]
    mine = piece(me)
    total = mine.astype(jnp.float32)
    for part in parts:
        total += part.astype(jnp.float32)
    return total.astype(mine.dtype)


def over_z(value, first):
    n = value.shape[0]
    turned = [[(k + first) % n for k in range(n)]]
    return lax.all_to_all(
        value, "z", split_axis=0, concat_axis=0, axis_index_groups=turned, tiled=True
    )


def pick(stack, index):
    return lax.dynamic_index_in_dim(stack, index, 0, keepdims=False)


def body(activations, weight_codes, block_scales, cotangent):
    f32, bf16 = jnp.float32, jnp.bfloat16
    c = lax.axis_index("c")
    y = lax.axis_index("y")
    x = lax.axis_index(X)
    tok, d_in = activations.shape
    own, cols = weight_codes.shape
    half = cols // 2
    rows = own // 4
    n_z = lax.axis_size("z")
    column = n_z * rows
    factor = float(tok * n_z * 32) ** (-0.5)

    other_act = lax.ppermute(activations, "c", SWAP)
    other_cot = lax.ppermute(cotangent, "c", SWAP)

    blocks = half // BLOCK
    codes = lax.dynamic_slice(weight_codes, (y * rows, c * half), (rows, half))
    scales = lax.dynamic_slice(block_scales, (y * rows, c * blocks), (rows, blocks))
    wide = jnp.repeat(scales.astype(f32), BLOCK, axis=1)
    mine = (codes.astype(f32) * wide).astype(bf16)
    spread = jnp.broadcast_to(mine[None], (n_z, rows, half))

    dims = (((0,), (0,)), ((), ()))
    acts = jnp.concatenate([activations, other_act], axis=0)
    cots = jnp.concatenate([cotangent, other_cot], axis=0)
    cots = lax.dynamic_slice(cots, (0, c * half), (2 * tok, half))
    grad = lax.dot_general(acts, cots, dims, preferred_element_type=f32)
    grad = (grad * factor).astype(bf16)
    grad = grad.reshape(2, n_z, 2, 4, rows, half)
    first = 11 * n_z // 16
    col = over_z(spread, first)

    def to_x(k):
        start = (k // 2, 0, k % 2, 0, 0, 0)
        return lax.dynamic_slice(grad, start, (1, n_z, 1, 4, rows, half)).reshape(n_z, 4, rows, half)

    line = spread_sum(to_x, X)
    plane = spread_sum(lambda k: lax.dynamic_index_in_dim(line, k, 1, keepdims=False), "y")
    col, plane = lax.optimization_barrier((col, plane))
    col = jnp.roll(col, first, axis=0)

    slab = jnp.broadcast_to(col.reshape(1, column, half), (4, column, half))
    slab = lax.all_to_all(slab, "y", split_axis=0, concat_axis=0, tiled=True)
    slab, plane = lax.optimization_barrier((slab, plane))
    held = [around(slab, X, shift) for shift in (2, 1, 3)]
    moved = over_z(jnp.roll(plane, n_z // 2, axis=0), n_z // 2)

    two, one, three = held
    stack = jnp.stack([slab, one, two, three])
    whole = jnp.stack([pick(stack, (x - k) % 4) for k in range(4)])
    whole = whole.reshape(2, 2, 4, n_z, rows, half)
    weight = whole.transpose(0, 3, 1, 2, 4, 5).reshape(d_in, half)

    proj = jnp.dot(acts, weight, preferred_element_type=f32).astype(bf16)
    got = lax.ppermute(proj[tok:], "c", SWAP)
    kept = proj[:tok]
    got, kept, moved = lax.optimization_barrier((got, kept, moved))
    piece = jnp.sum(moved.astype(f32), axis=0)
    pieces = jnp.broadcast_to(piece[None], (8, rows, half))
    pieces = lax.all_to_all(pieces, ("y", "c"), split_axis=0, concat_axis=0, tiled=True)
    pieces = pieces.reshape(4, 2, rows, half)
    weight_grads = pieces.transpose(0, 2, 1, 3).reshape(own, cols)

    left = jnp.where(c == 0, kept, got)
    right = jnp.where(c == 0, got, kept)
    projected = jnp.concatenate([left, right], axis=1)
    return (projected, weight_grads)


def solution(mesh):
    fine = Mesh(mesh.devices.reshape(2, 32, 2, 4, 2), ALL)
    placed = (
        P(ALL, None),
        P(("xh", "z", "xl"), None),
        P(("xh", "z", "xl"), None),
        P(ALL, None),
    )
    return jax.shard_map(
        body,
        mesh=fine,
        in_specs=placed,
        out_specs=(P(ALL, None), P(("xh", "z", "xl"), None)),
        check_vma=False,
    )
```

```python
import jax
import jax.numpy as jnp
from jax import lax
from jax.sharding import Mesh, PartitionSpec as P

BLOCK = 128
ALL = ("xh", "z", "xl", "y", "c")
X = ("xh", "xl")
SWAP = [(0, 1), (1, 0)]


def around(value, axes, shift):
    return lax.ppermute(value, axes, [(i, (i + shift) % 4) for i in range(4)])


def spread_sum(piece, axes):
    me = lax.axis_index(axes)
    parts = [around(piece((me + shift) % 4), axes, shift) for shift in (2, 1, 3)]
    mine = piece(me)
    total = mine.astype(jnp.float32)
    for part in parts:
        total += part.astype(jnp.float32)
    return total.astype(mine.dtype)


def over_z(value, first):
    n = value.shape[0]
    turned = [[(k + first) % n for k in range(n)]]
    return lax.all_to_all(
        value, "z", split_axis=0, concat_axis=0, axis_index_groups=turned, tiled=True
    )


def pick(stack, index):
    return lax.dynamic_index_in_dim(stack, index, 0, keepdims=False)


def body(activations, weight_codes, block_scales, cotangent):
    f32, bf16 = jnp.float32, jnp.bfloat16
    c = lax.axis_index("c")
    y = lax.axis_index("y")
    x = lax.axis_index(X)
    tok, d_in = activations.shape
    own, cols = weight_codes.shape
    half = cols // 2
    rows = own // 4
    n_z = lax.axis_size("z")
    column = n_z * rows
    factor = float(tok * n_z * 32) ** (-0.5)

    other_act = lax.ppermute(activations, "c", SWAP)
    other_cot = lax.ppermute(cotangent, "c", SWAP)

    blocks = half // BLOCK
    codes = lax.dynamic_slice(weight_codes, (y * rows, c * half), (rows, half))
    scales = lax.dynamic_slice(block_scales, (y * rows, c * blocks), (rows, blocks))
    wide = jnp.repeat(scales.astype(f32), BLOCK, axis=1)
    mine = (codes.astype(f32) * wide).astype(bf16)
    spread = jnp.broadcast_to(mine[None], (n_z, rows, half))

    dims = (((0,), (0,)), ((), ()))
    acts = jnp.concatenate([activations, other_act], axis=0)
    cots = jnp.concatenate([cotangent, other_cot], axis=0)
    cots = lax.dynamic_slice(cots, (0, c * half), (2 * tok, half))
    grad = lax.dot_general(acts, cots, dims, preferred_element_type=f32)
    grad = (grad * factor).astype(bf16)
    grad = grad.reshape(2, n_z, 2, 4, rows, half)
    first = 11 * n_z // 16
    col = over_z(spread, first)

    def to_x(k):
        start = (k // 2, 0, k % 2, 0, 0, 0)
        return lax.dynamic_slice(grad, start, (1, n_z, 1, 4, rows, half)).reshape(n_z, 4, rows, half)

    line = spread_sum(to_x, X)
    plane = spread_sum(lambda k: lax.dynamic_index_in_dim(line, k, 1, keepdims=False), "y")
    col, plane = lax.optimization_barrier((col, plane))
    col = jnp.roll(col, first, axis=0)

    slab = jnp.broadcast_to(col.reshape(1, column, half), (4, column, half))
    slab = lax.all_to_all(slab, "y", split_axis=0, concat_axis=0, tiled=True)
    plane = jnp.roll(plane, n_z // 2, axis=0)
    slab, plane = lax.optimization_barrier((slab, plane))
    held = [around(slab, X, shift) for shift in (2, 1, 3)]
    moved = over_z(plane, n_z // 2)

    two, one, three = held
    stack = jnp.stack([slab, one, two, three])
    whole = jnp.stack([pick(stack, (x - k) % 4) for k in range(4)])
    whole = whole.reshape(2, 2, 4, n_z, rows, half)
    weight = whole.transpose(0, 3, 1, 2, 4, 5).reshape(d_in, half)

    proj = jnp.dot(acts, weight, preferred_element_type=f32).astype(bf16)
    got = lax.ppermute(proj[tok:], "c", SWAP)
    kept = proj[:tok]
    got, kept, moved = lax.optimization_barrier((got, kept, moved))
    piece = jnp.sum(moved.astype(f32), axis=0)
    pieces = jnp.broadcast_to(piece[None], (8, rows, half))
    pieces = lax.all_to_all(pieces, ("y", "c"), split_axis=0, concat_axis=0, tiled=True)
    pieces = pieces.reshape(4, 2, rows, half)
    weight_grads = pieces.transpose(0, 2, 1, 3).reshape(own, cols)

    left = jnp.where(c == 0, kept, got)
    right = jnp.where(c == 0, got, kept)
    projected = jnp.concatenate([left, right], axis=1)
    return (projected, weight_grads)


def solution(mesh):
    fine = Mesh(mesh.devices.reshape(2, 32, 2, 4, 2), ALL)
    placed = (
        P(ALL, None),
        P(("xh", "z", "xl"), None),
        P(("xh", "z", "xl"), None),
        P(ALL, None),
    )
    return jax.shard_map(
        body,
        mesh=fine,
        in_specs=placed,
        out_specs=(P(ALL, None), P(("xh", "z", "xl"), None)),
        check_vma=False,
    )
```

```python
import jax
import jax.numpy as jnp
from jax import lax
from jax.sharding import Mesh, PartitionSpec as P

BLOCK = 128
ALL = ("xh", "z", "xl", "y", "c")
X = ("xh", "xl")
SWAP = [(0, 1), (1, 0)]


def around(value, axes, shift):
    return lax.ppermute(value, axes, [(i, (i + shift) % 4) for i in range(4)])


def spread_sum(piece, axes):
    me = lax.axis_index(axes)
    parts = [around(piece((me + shift) % 4), axes, shift) for shift in (2, 1, 3)]
    mine = piece(me)
    total = mine.astype(jnp.float32)
    for part in parts:
        total += part.astype(jnp.float32)
    return total.astype(mine.dtype)


def over_z(value, first):
    n = value.shape[0]
    turned = [[(k + first) % n for k in range(n)]]
    return lax.all_to_all(
        value, "z", split_axis=0, concat_axis=0, axis_index_groups=turned, tiled=True
    )


def pick(stack, index):
    return lax.dynamic_index_in_dim(stack, index, 0, keepdims=False)


def body(activations, weight_codes, block_scales, cotangent):
    f32, bf16 = jnp.float32, jnp.bfloat16
    c = lax.axis_index("c")
    y = lax.axis_index("y")
    x = lax.axis_index(X)
    tok, d_in = activations.shape
    own, cols = weight_codes.shape
    half = cols // 2
    rows = own // 4
    n_z = lax.axis_size("z")
    column = n_z * rows
    factor = float(tok * n_z * 32) ** (-0.5)

    other_act = lax.ppermute(activations, "c", SWAP)
    other_cot = lax.ppermute(cotangent, "c", SWAP)

    blocks = half // BLOCK
    codes = lax.dynamic_slice(weight_codes, (y * rows, c * half), (rows, half))
    scales = lax.dynamic_slice(block_scales, (y * rows, c * blocks), (rows, blocks))
    wide = jnp.repeat(scales.astype(f32), BLOCK, axis=1)
    mine = (codes.astype(f32) * wide).astype(bf16)
    spread = jnp.broadcast_to(mine[None], (n_z, rows, half))

    dims = (((0,), (0,)), ((), ()))
    acts = jnp.concatenate([activations, other_act], axis=0)
    cots = jnp.concatenate([cotangent, other_cot], axis=0)
    cots = lax.dynamic_slice(cots, (0, c * half), (2 * tok, half))
    grad = lax.dot_general(acts, cots, dims, preferred_element_type=f32)
    grad = (grad * factor).astype(bf16)
    grad = grad.reshape(2, n_z, 2, 4, rows, half)
    first = 11 * n_z // 16
    col = over_z(spread, first)

    def to_x(k):
        start = (k // 2, 0, k % 2, 0, 0, 0)
        return lax.dynamic_slice(grad, start, (1, n_z, 1, 4, rows, half)).reshape(n_z, 4, rows, half)

    line = spread_sum(to_x, X)
    plane = spread_sum(lambda k: lax.dynamic_index_in_dim(line, k, 1, keepdims=False), "y")
    col, plane = lax.optimization_barrier((col, plane))
    col = jnp.roll(col, first, axis=0)

    slab = jnp.broadcast_to(col.reshape(1, column, half), (4, column, half))
    slab = lax.all_to_all(slab, "y", split_axis=0, concat_axis=0, tiled=True)
    slab, plane = lax.optimization_barrier((slab, plane))
    held = [around(slab, X, shift) for shift in (1, 3, 2)]
    moved = over_z(jnp.roll(plane, n_z // 2, axis=0), n_z // 2)

    one, three, two = held
    stack = jnp.stack([slab, one, two, three])
    whole = jnp.stack([pick(stack, (x - k) % 4) for k in range(4)])
    whole = whole.reshape(2, 2, 4, n_z, rows, half)
    weight = whole.transpose(0, 3, 1, 2, 4, 5).reshape(d_in, half)

    proj = jnp.dot(acts, weight, preferred_element_type=f32).astype(bf16)
    got = lax.ppermute(proj[tok:], "c", SWAP)
    kept = proj[:tok]
    got, kept, moved = lax.optimization_barrier((got, kept, moved))
    piece = jnp.sum(moved.astype(f32), axis=0)
    pieces = jnp.broadcast_to(piece[None], (8, rows, half))
    pieces = lax.all_to_all(pieces, ("y", "c"), split_axis=0, concat_axis=0, tiled=True)
    pieces = pieces.reshape(4, 2, rows, half)
    weight_grads = pieces.transpose(0, 2, 1, 3).reshape(own, cols)

    left = jnp.where(c == 0, kept, got)
    right = jnp.where(c == 0, got, kept)
    projected = jnp.concatenate([left, right], axis=1)
    return (projected, weight_grads)


def solution(mesh):
    fine = Mesh(mesh.devices.reshape(2, 32, 2, 4, 2), ALL)
    placed = (
        P(ALL, None),
        P(("xh", "z", "xl"), None),
        P(("xh", "z", "xl"), None),
        P(ALL, None),
    )
    return jax.shard_map(
        body,
        mesh=fine,
        in_specs=placed,
        out_specs=(P(ALL, None), P(("xh", "z", "xl"), None)),
        check_vma=False,
    )
```
